512 devices in a mesh: rep: 32 (over z, y_lo), tp: 16 (over x, y_hi, core).
Axes of the slice: x: 4, y: 4 (y_hi: 2, y_lo: 2; y = y_hi * 2 + y_lo), z: 16, core: 2. Of those that a mesh axis runs over, the one named last changes fastest.
Arguments:
- step_index: int32 [1], replicated, may hold values from 0 to 63
- tokens: bfloat16 [4096, 8192], P('rep', 'tp'), may hold values from -6 to 6
- cotangent: bfloat16 [4096, 1024], P('rep', 'tp'), may hold values from -6 to 6
- weights: float32 [32, 1024, 8192], P('rep', 'tp'), may hold values from -0.0625 to 0.0625
Outputs:
- new_weights: float32 [32, 1024, 8192], P('rep', 'tp')
- keys: bfloat16 [4096, 1024], P('rep', 'tp')
- input_grad: bfloat16 [4096, 8192], P('rep', 'tp')
The draws below stay inside these ranges and needn't reach their ends.
All inputs are finite; a program needn't handle non-finite values.
Results may differ from the reference program's by a relative error of at most 0.0065.
Values may be sent and summed in bfloat16 or wider, within the bound.
A program may use at most 64 MiB of HBM per device.

```python
import jax
import jax.numpy as jnp
from jax import lax

D = 8192
KVD = 1024
TOK = 128
TOKENS = 4096
N_REP = 32


def block_levels(own_key, shape, split, least, high):
    loudness = 1.0
    for position, parts in split:
        draws = jax.random.uniform(jax.random.fold_in(jax.random.fold_in(own_key, 6), position), (parts,), jnp.float32, least / len(split), high / len(split))
        loudness = loudness * jnp.repeat(jnp.exp(draws), shape[position] // parts).reshape((-1,) + (1,) * (len(shape) - 1 - position))
    return loudness


def bell_draw(key, dims, spread, limit, shards=(), kind=jnp.bfloat16):
    entries = jax.random.normal(key, dims, jnp.float32) * spread
    if len(shards) > 0:
        entries = block_levels(key, dims, shards, -0.22, 0.18) * entries
    return jnp.clip(entries, min=-limit, max=limit).astype(kind)


def setup_inputs(seed: int = 0) -> dict:
    seeds = jax.random.split(jax.random.key(seed), 5)
    step_index = jax.random.randint(seeds[0], (1,), 0, 64).astype(jnp.int32)
    tokens = bell_draw(seeds[1], (TOKENS, D), 1.0, 6.0, ((0, 32), (1, 16)))
    cotangent = bell_draw(seeds[2], (TOKENS, KVD), 1.0, 6.0, ((0, 32), (1, 16)))
    weights = bell_draw(seeds[3], (N_REP, KVD, D), D ** -0.5, 0.0625, ((0, 32), (1, 16)), jnp.float32)
    return {"step_index": step_index, "tokens": tokens, "cotangent": cotangent, "weights": weights}


LEARNING = 0.01


def reference(step_index, tokens, cotangent, weights):
    bits = N_REP.bit_length() - 1
    chosen = jnp.remainder(step_index[0], bits).astype(jnp.int32)
    stride = jnp.left_shift(jnp.int32(1), chosen)
    rate = LEARNING * (jnp.remainder(step_index[0], 64) + 1).astype(jnp.float32) / 64.0
    rows = tokens.reshape(N_REP, TOK, D)
    grads = cotangent.reshape(N_REP, TOK, KVD)

    def one_replica(item):
        replica, token_rows, grad_rows = item
        partner = jnp.bitwise_xor(replica, stride).astype(jnp.int32)
        mine = lax.dynamic_index_in_dim(weights, replica, 0, keepdims=False)
        theirs = lax.dynamic_index_in_dim(weights, partner, 0, keepdims=False)
        averaged = 0.5 * (mine + theirs)
        cast = averaged.astype(jnp.bfloat16)
        keys = jnp.dot(token_rows, cast.T, preferred_element_type=jnp.float32).astype(jnp.bfloat16)
        input_grad = jnp.dot(grad_rows, cast, preferred_element_type=jnp.float32).astype(jnp.bfloat16)
        grad = jnp.dot(grad_rows.T, token_rows, preferred_element_type=jnp.float32)
        return averaged - rate * grad, keys, input_grad

    replicas = jnp.arange(N_REP, dtype=jnp.int32)
    new_weights, keys, input_grad = lax.map(one_replica, (replicas, rows, grads))
    return new_weights, keys.reshape(TOKENS, KVD), input_grad.reshape(TOKENS, D)
```

```python
from functools import partial

import jax
import jax.numpy as jnp
from jax import lax
from jax.experimental import pallas as pl
from jax.experimental.pallas import tpu as pltpu
from jax.sharding import PartitionSpec as P

LEARNING = 0.01
MESH = pl.DeviceIdType.MESH
LANES = 128
AHEAD = 5


def flip(index, other, bits):
    out = 0
    for k in range(bits):
        a = lax.rem(lax.div(index, 2**k), 2)
        b = (other // 2**k) % 2 if isinstance(other, int) else lax.rem(lax.div(other, 2**k), 2)
        out = out + (a + b - 2 * a * b) * 2**k
    return out


def kernel(
    bit,
    step_ref,
    tok_ref,
    cot_ref,
    w_ref,
    nw_ref,
    keys_ref,
    ig_ref,
    wbuf,
    zsend,
    zrecv,
    cast,
    arecv,
    packs,
    cot,
    keys_acc,
    ig_acc,
    w_sem,
    o_sem,
    t_in,
    zs_sem,
    zr_sem,
    as_sem,
    ar_sem,
    ts_sem,
    tr_sem,
):
    blocks, features, width = wbuf.shape
    tok = tok_ref.shape[0]
    pieces = width // LANES
    piece = features // pieces
    tp = lax.axis_index("tp")
    rep = lax.axis_index("rep")
    tp_bits = blocks.bit_length() - 1
    rep_bits = lax.axis_size("rep").bit_length() - 1
    partner = {"rep": flip(rep, 2**bit, rep_bits)}

    def peer(m):
        return {"tp": flip(tp, m, tp_bits)}

    def columns(m):
        return pl.ds(pl.multiple_of(flip(tp, m, tp_bits) * width, width), width)

    def load(m):
        return pltpu.make_async_copy(w_ref.at[0, :, columns(m)], wbuf.at[m], w_sem.at[m])

    def store(m):
        return pltpu.make_async_copy(wbuf.at[m], nw_ref.at[0, :, columns(m)], o_sem.at[m])

    def exchange(m):
        return pltpu.make_async_remote_copy(
            zsend.at[m], zrecv.at[m], zs_sem.at[m], zr_sem.at[m], device_id=partner, device_id_type=MESH
        )

    def scatter(m):
        return pltpu.make_async_remote_copy(
            cast.at[m], arecv.at[m], as_sem.at[m], ar_sem.at[m], device_id=peer(m), device_id_type=MESH
        )

    def pass_on(source, via):
        land = flip(source, via, tp_bits) if not isinstance(source, int) else source ^ via
        return pltpu.make_async_remote_copy(
            packs.at[source], packs.at[land], ts_sem.at[land], tr_sem.at[land], device_id=peer(via), device_id_type=MESH
        )

    tok_in = pltpu.make_async_copy(tok_ref, packs.at[0, pl.ds(0, tok), :], t_in.at[0])
    cot_in = pltpu.make_async_copy(cot_ref, cot, t_in.at[1])
    last = blocks - 1

    @pl.loop(0, blocks)
    def _(i):
        load(last - i).start()

    tok_in.start()
    cot_in.start()

    barrier = pltpu.get_barrier_semaphore()
    pl.semaphore_signal(barrier, inc=1, device_id=partner, device_id_type=MESH)

    @pl.loop(1, blocks)
    def _(m):
        pl.semaphore_signal(barrier, inc=1, device_id=peer(m), device_id_type=MESH)

    def prepare(m):
        load(m).wait()
        zsend[m] = wbuf[m].astype(jnp.bfloat16)

    @pl.loop(0, AHEAD)
    def _(i):
        prepare(last - i)

    pl.semaphore_wait(barrier, blocks)

    @pl.loop(0, AHEAD)
    def _(i):
        exchange(last - i).start()

    tok_in.wait()
    cot_in.wait()
    for k in range(pieces):
        packs[0, pl.ds(tok, piece), pl.ds(k * LANES, LANES)] = cot[pl.ds(k * piece, piece), :]
    for via in (2, 12, 8, 4, 1):
        pass_on(0, via).start()
    keys_acc[...] = jnp.zeros_like(keys_acc)
    ig_acc[...] = jnp.zeros_like(ig_acc)
    rate = LEARNING * (lax.rem(step_ref[0], 64) + 1).astype(jnp.float32) * (1.0 / 64.0)

    def average(i):
        m = last - i

        @pl.when(i + AHEAD < blocks)
        def _():
            prepare(m - AHEAD)
            exchange(m - AHEAD).start()

        exchange(m).wait_recv()
        mean = 0.5 * (wbuf[m] + zrecv[m].astype(jnp.float32))
        wbuf[m] = mean
        cast[m] = mean.astype(jnp.bfloat16)

        @pl.when(m > 0)
        def _():
            scatter(m).start()

    def project(m):
        block = packs[m, pl.ds(0, tok), :]
        keys_acc[...] += lax.dot_general(
            cast[m], block, (((1,), (1,)), ((), ())), preferred_element_type=jnp.float32
        )
        grad = jnp.dot(cot[...], block, preferred_element_type=jnp.float32)
        wbuf[m] = wbuf[m] - rate * grad
        store(m).start()

    def back(low):
        parts = []
        for q in range(4):
            for k in range(pieces):
                parts.append(packs[low + q, pl.ds(tok, piece), pl.ds(k * LANES, LANES)])
        left = jnp.concatenate(parts, axis=0)
        right = arecv[pl.ds(low, 4)].reshape(4 * features, width)
        ig_acc[...] += lax.dot_general(
            left, right, (((0,), (0,)), ((), ())), preferred_element_type=jnp.float32
        )

    half = blocks // 2

    @pl.loop(0, half)
    def _(i):
        average(i)

        @pl.when(i == 0)
        def _():
            pass_on(0, 2).wait_recv()
            for via in (12, 8, 4, 1):
                pass_on(2, via).start()

        @pl.when((i >= 1) & (i <= 6))
        def _():
            r = i - 1
            source = 4 * (lax.rem(r, 3) + 1) + 2 * lax.div(r, 3)
            arrived = pltpu.make_async_remote_copy(
                packs.at[source], packs.at[source], ts_sem.at[source], tr_sem.at[source],
                device_id=peer(1), device_id_type=MESH,
            )
            arrived.wait_recv()
            pass_on(source, 1).start()

    @pl.loop(half, blocks)
    def _(i):
        average(i)
        m = last - 2 * (i - half)
        pltpu.make_async_remote_copy(
            packs.at[m], packs.at[m], ts_sem.at[m], tr_sem.at[m], device_id=peer(1), device_id_type=MESH
        ).wait_recv()
        project(m)
        project(m - 1)

        @pl.when((i >= 10) & (lax.rem(i, 2) == 0))
        def _():
            low = 12 - 4 * lax.div(i - 10, 2)
            for q in range(4):
                scatter(low + q).wait_recv()
            back(low)

    arecv[0] = cast[0]
    for q in range(1, 4):
        scatter(q).wait_recv()
    back(0)
    ig_ref[...] = ig_acc[...].astype(ig_ref.dtype)
    keys_ref[...] = keys_acc[...].astype(keys_ref.dtype)

    @pl.loop(0, blocks)
    def _(m):
        exchange(m).wait_send()
        store(m).wait()

        @pl.when(m > 0)
        def _():
            scatter(m).wait_send()
            pltpu.make_async_remote_copy(
                packs.at[m], packs.at[m], ts_sem.at[m], tr_sem.at[m], device_id=peer(1), device_id_type=MESH
            ).wait_send()


def level(step_index, tokens, cot_t, weights, bit):
    blocks = lax.axis_size("tp")
    tok, width = tokens.shape
    features = cot_t.shape[0]
    rows = tok + features * LANES // width
    bf16, f32 = jnp.bfloat16, jnp.float32
    dma = pltpu.SemaphoreType.DMA((blocks,))
    hbm = pl.BlockSpec(memory_space=pl.ANY)
    vmem = pl.BlockSpec(memory_space=pltpu.VMEM)
    return pl.pallas_call(
        partial(kernel, bit),
        out_shape=(
            jax.ShapeDtypeStruct(weights.shape, f32),
            jax.ShapeDtypeStruct(cot_t.shape, bf16),
            jax.ShapeDtypeStruct(tokens.shape, bf16),
        ),
        in_specs=[pl.BlockSpec(memory_space=pltpu.SMEM), hbm, hbm, hbm],
        out_specs=(hbm, vmem, vmem),
        scratch_shapes=[
            pltpu.VMEM((blocks, features, width), f32),
            pltpu.VMEM((blocks, features, width), bf16),
            pltpu.VMEM((blocks, features, width), bf16),
            pltpu.VMEM((blocks, features, width), bf16),
            pltpu.VMEM((blocks, features, width), bf16),
            pltpu.VMEM((blocks, rows, width), bf16),
            pltpu.VMEM((features, tok), bf16),
            pltpu.VMEM((features, tok), f32),
            pltpu.VMEM((tok, width), f32),
            dma,
            dma,
            pltpu.SemaphoreType.DMA((2,)),
            dma,
            dma,
            dma,
            dma,
            dma,
            dma,
        ],
        compiler_params=pltpu.CompilerParams(
            collective_id=bit, has_side_effects=True, vmem_limit_bytes=32 * 2**20
        ),
    )(step_index, tokens, cot_t, weights)


def local(step_index, tokens, cotangent, weights):
    bits = lax.axis_size("rep").bit_length() - 1
    chosen = jnp.remainder(step_index[0], bits)
    branches = [partial(level, bit=bit) for bit in range(bits)]
    new_weights, keys_t, input_grad = lax.switch(chosen, branches, step_index, tokens, cotangent.T, weights)
    return (new_weights, keys_t.T, input_grad)


def solution(mesh):
    in_specs = (P(), P("rep", "tp"), P("rep", "tp"), P("rep", "tp", None))
    out_specs = (P("rep", "tp", None), P("rep", "tp"), P("rep", "tp"))
    return jax.shard_map(local, mesh=mesh, in_specs=in_specs, out_specs=out_specs, check_vma=False)
```

```python
from functools import partial

import jax
import jax.numpy as jnp
from jax import lax
from jax.experimental import pallas as pl
from jax.experimental.pallas import tpu as pltpu
from jax.sharding import PartitionSpec as P

LEARNING = 0.01
MESH = pl.DeviceIdType.MESH
LANES = 128
AHEAD = 8
RELAYS = ((2, (12, 4, 1)), (12, (4, 1)), (4, (1,)), (6, (12, 1)), (14, (1,)), (8, (1,)), (10, (1,)))
RELAY_STEPS = (3, 4, 5, 7, 8, 9, 10)


def flip(index, other, bits):
    out = 0
    for k in range(bits):
        a = lax.rem(lax.div(index, 2**k), 2)
        b = (other // 2**k) % 2 if isinstance(other, int) else lax.rem(lax.div(other, 2**k), 2)
        out = out + (a + b - 2 * a * b) * 2**k
    return out


def kernel(
    bit,
    step_ref,
    tok_ref,
    cot_ref,
    w_ref,
    nw_ref,
    keys_ref,
    ig_ref,
    wbuf,
    zsend,
    zrecv,
    cast,
    arecv,
    packs,
    cot,
    keys_acc,
    ig_acc,
    w_sem,
    o_sem,
    t_in,
    zs_sem,
    zr_sem,
    as_sem,
    ar_sem,
    ts_sem,
    tr_sem,
    go_sem,
    all_sem,
):
    blocks, features, width = wbuf.shape
    tok = tok_ref.shape[0]
    pieces = width // LANES
    piece = features // pieces
    tp = lax.axis_index("tp")
    rep = lax.axis_index("rep")
    tp_bits = blocks.bit_length() - 1
    rep_bits = lax.axis_size("rep").bit_length() - 1
    other = flip(rep, 2**bit, rep_bits)
    partner = {"rep": other}

    def peer(m):
        return {"tp": flip(tp, m, tp_bits)}

    def columns(m):
        return pl.ds(pl.multiple_of(flip(tp, m, tp_bits) * width, width), width)

    def load(m):
        return pltpu.make_async_copy(w_ref.at[0, :, columns(m)], wbuf.at[m], w_sem.at[m])

    def store(m):
        return pltpu.make_async_copy(wbuf.at[m], nw_ref.at[0, :, columns(m)], o_sem.at[m])

    def exchange(m):
        return pltpu.make_async_remote_copy(
            zsend.at[m], zrecv.at[m], zs_sem.at[m], zr_sem.at[m], device_id=partner, device_id_type=MESH
        )

    def scatter(m):
        owner = peer(m)
        if bit == 0:
            owner["rep"] = rep + lax.rem(lax.div(jnp.int32(m), 2), 2) * (other - rep)
        return pltpu.make_async_remote_copy(
            cast.at[m], arecv.at[m], as_sem.at[m], ar_sem.at[m], device_id=owner, device_id_type=MESH
        )

    def pass_on(source, via):
        land = flip(source, via, tp_bits) if not isinstance(source, int) else source ^ via
        return pltpu.make_async_remote_copy(
            packs.at[source], packs.at[land], ts_sem.at[land], tr_sem.at[land], device_id=peer(via), device_id_type=MESH
        )

    def arrival(m):
        return pltpu.make_async_remote_copy(
            packs.at[m], packs.at[m], ts_sem.at[m], tr_sem.at[m], device_id=peer(1), device_id_type=MESH
        )

    tok_in = pltpu.make_async_copy(tok_ref, packs.at[0, pl.ds(0, tok), :], t_in.at[0])
    cot_in = pltpu.make_async_copy(cot_ref, cot, t_in.at[1])
    last = blocks - 1

    @pl.loop(0, blocks)
    def _(i):
        load(last - i).start()

    tok_in.start()
    cot_in.start()

    barrier = pltpu.get_barrier_semaphore()
    pl.semaphore_signal(barrier, inc=1, device_id=partner, device_id_type=MESH)

    @pl.when(tp != 0)
    def _():
        pl.semaphore_signal(barrier, inc=1, device_id={"tp": 0}, device_id_type=MESH)

    def prepare(m):
        load(m).wait()
        zsend[m] = wbuf[m].astype(jnp.bfloat16)

    @pl.loop(0, AHEAD)
    def _(i):
        prepare(last - i)

    @pl.when(tp != 0)
    def _():
        pl.semaphore_wait(barrier, 1)

    @pl.when(tp == 0)
    def _():
        pl.semaphore_wait(barrier, blocks)
        if bit == 0:
            pl.semaphore_signal(all_sem, inc=1, device_id=partner, device_id_type=MESH)

    @pl.loop(0, AHEAD)
    def _(i):
        exchange(last - i).start()

    @pl.when(tp == 0)
    def _():
        if bit == 0:
            pl.semaphore_wait(all_sem, 1)

        @pl.loop(1, blocks)
        def _(t):
            pl.semaphore_signal(go_sem, inc=1, device_id={"tp": t}, device_id_type=MESH)

    tok_in.wait()
    cot_in.wait()
    for k in range(pieces):
        packs[0, pl.ds(tok, piece), pl.ds(k * LANES, LANES)] = cot[pl.ds(k * piece, piece), :]

    @pl.when(tp != 0)
    def _():
        pl.semaphore_wait(go_sem, 1)

    for via in (2, 12, 4, 1):
        pass_on(0, via).start()
    keys_acc[...] = jnp.zeros_like(keys_acc)
    ig_acc[...] = jnp.zeros_like(ig_acc)
    rate = LEARNING * (lax.rem(step_ref[0], 64) + 1).astype(jnp.float32) * (1.0 / 64.0)

    def average(i):
        m = last - i

        @pl.when(i + AHEAD < blocks)
        def _():
            prepare(m - AHEAD)
            exchange(m - AHEAD).start()

        exchange(m).wait_recv()
        mean = 0.5 * (wbuf[m] + zrecv[m].astype(jnp.float32))
        wbuf[m] = mean
        cast[m] = mean.astype(jnp.bfloat16)

        @pl.when(m > 0)
        def _():
            scatter(m).start()

    def project(m):
        block = packs[m, pl.ds(0, tok), :]
        keys_acc[...] += lax.dot_general(
            cast[m], block, (((1,), (1,)), ((), ())), preferred_element_type=jnp.float32
        )
        grad = jnp.dot(cot[...], block, preferred_element_type=jnp.float32)
        wbuf[m] = wbuf[m] - rate * grad
        store(m).start()

    def back(low):
        parts = []
        for q in range(4):
            for k in range(pieces):
                parts.append(packs[low + q, pl.ds(tok, piece), pl.ds(k * LANES, LANES)])
        left = jnp.concatenate(parts, axis=0)
        right = arecv[pl.ds(low, 4)].reshape(4 * features, width)
        ig_acc[...] += lax.dot_general(
            left, right, (((0,), (0,)), ((), ())), preferred_element_type=jnp.float32
        )

    @pl.loop(0, blocks)
    def _(i):
        average(i)
        for at, (source, vias) in zip(RELAY_STEPS, RELAYS):

            @pl.when(i == at)
            def _(source=source, vias=vias):
                arrival(source).wait_recv()
                for via in vias:
                    pass_on(source, via).start()

        @pl.when(i >= 12)
        def _():
            low = 4 * (last - i)
            arrival(low + 3).wait_recv()
            project(low + 3)
            project(low + 2)
            arrival(low + 1).wait_recv()
            project(low + 1)
            project(low)

        @pl.when(i >= 13)
        def _():
            low = 4 * (blocks - i)
            for q in range(4):
                scatter(low + q).wait_recv()
            back(low)

    arecv[0] = cast[0]
    for q in range(1, 4):
        scatter(q).wait_recv()
    back(0)
    ig_ref[...] = ig_acc[...].astype(ig_ref.dtype)
    keys_ref[...] = keys_acc[...].astype(keys_ref.dtype)

    @pl.loop(0, blocks)
    def _(m):
        exchange(m).wait_send()
        store(m).wait()

        @pl.when(m > 0)
        def _():
            scatter(m).wait_send()
            arrival(m).wait_send()


def level(step_index, tokens, cot_t, weights, bit):
    blocks = lax.axis_size("tp")
    tok, width = tokens.shape
    features = cot_t.shape[0]
    rows = tok + features * LANES // width
    bf16, f32 = jnp.bfloat16, jnp.float32
    dma = pltpu.SemaphoreType.DMA((blocks,))
    hbm = pl.BlockSpec(memory_space=pl.ANY)
    vmem = pl.BlockSpec(memory_space=pltpu.VMEM)
    return pl.pallas_call(
        partial(kernel, bit),
        out_shape=(
            jax.ShapeDtypeStruct(weights.shape, f32),
            jax.ShapeDtypeStruct(cot_t.shape, bf16),
            jax.ShapeDtypeStruct(tokens.shape, bf16),
        ),
        in_specs=[pl.BlockSpec(memory_space=pltpu.SMEM), hbm, hbm, hbm],
        out_specs=(hbm, vmem, vmem),
        scratch_shapes=[
            pltpu.VMEM((blocks, features, width), f32),
            pltpu.VMEM((blocks, features, width), bf16),
            pltpu.VMEM((blocks, features, width), bf16),
            pltpu.VMEM((blocks, features, width), bf16),
            pltpu.VMEM((blocks, features, width), bf16),
            pltpu.VMEM((blocks, rows, width), bf16),
            pltpu.VMEM((features, tok), bf16),
            pltpu.VMEM((features, tok), f32),
            pltpu.VMEM((tok, width), f32),
            dma,
            dma,
            pltpu.SemaphoreType.DMA((2,)),
            dma,
            dma,
            dma,
            dma,
            dma,
            dma,
            pltpu.SemaphoreType.REGULAR,
            pltpu.SemaphoreType.REGULAR,
        ],
        compiler_params=pltpu.CompilerParams(
            collective_id=bit, has_side_effects=True, vmem_limit_bytes=32 * 2**20
        ),
    )(step_index, tokens, cot_t, weights)


def local(step_index, tokens, cotangent, weights):
    bits = lax.axis_size("rep").bit_length() - 1
    chosen = jnp.remainder(step_index[0], bits)
    branches = [partial(level, bit=bit) for bit in range(bits)]
    new_weights, keys_t, input_grad = lax.switch(chosen, branches, step_index, tokens, cotangent.T, weights)
    return (new_weights, keys_t.T, input_grad)


def solution(mesh):
    in_specs = (P(), P("rep", "tp"), P("rep", "tp"), P("rep", "tp", None))
    out_specs = (P("rep", "tp", None), P("rep", "tp"), P("rep", "tp"))
    return jax.shard_map(local, mesh=mesh, in_specs=in_specs, out_specs=out_specs, check_vma=False)
```

```python
from functools import partial

import jax
import jax.numpy as jnp
from jax import lax
from jax.experimental import pallas as pl
from jax.experimental.pallas import tpu as pltpu
from jax.sharding import PartitionSpec as P

LEARNING = 0.01
MESH = pl.DeviceIdType.MESH
LANES = 128
AHEAD = 8
RELAYS = ((2, (12, 4, 1)), (12, (4, 1)), (4, (1,)), (6, (12, 1)), (14, (1,)), (8, (1,)), (10, (1,)))
RELAY_STEPS = (3, 4, 5, 7, 8, 9, 10)


def flip(index, other, bits):
    out = 0
    for k in range(bits):
        a = lax.rem(lax.div(index, 2**k), 2)
        b = (other // 2**k) % 2 if isinstance(other, int) else lax.rem(lax.div(other, 2**k), 2)
        out = out + (a + b - 2 * a * b) * 2**k
    return out


def backwards(slot, bits):
    return sum(lax.rem(lax.div(jnp.int32(slot), 2**k), 2) * 2 ** (bits - 1 - k) for k in range(bits))


def kernel(
    bit,
    step_ref,
    tok_ref,
    cot_ref,
    w_ref,
    nw_ref,
    keys_ref,
    ig_ref,
    wbuf,
    zsend,
    zrecv,
    cast,
    arecv,
    packs,
    cot,
    keys_acc,
    ig_acc,
    w_sem,
    o_sem,
    t_in,
    zs_sem,
    zr_sem,
    as_sem,
    ar_sem,
    ts_sem,
    tr_sem,
    go_sem,
    all_sem,
):
    blocks, features, width = wbuf.shape
    tok = tok_ref.shape[0]
    pieces = width // LANES
    piece = features // pieces
    tp = lax.axis_index("tp")
    rep = lax.axis_index("rep")
    tp_bits = blocks.bit_length() - 1
    rep_bits = lax.axis_size("rep").bit_length() - 1
    other = flip(rep, 2**bit, rep_bits)
    partner = {"rep": other}

    def peer(m):
        return {"tp": flip(tp, m, tp_bits)}

    def columns(s):
        return pl.ds(pl.multiple_of(flip(tp, backwards(s, tp_bits), tp_bits) * width, width), width)

    def load(m):
        return pltpu.make_async_copy(w_ref.at[0, :, columns(m)], wbuf.at[m], w_sem.at[m])

    def store(m):
        return pltpu.make_async_copy(wbuf.at[m], nw_ref.at[0, :, columns(m)], o_sem.at[m])

    def exchange(m):
        return pltpu.make_async_remote_copy(
            zsend.at[m], zrecv.at[m], zs_sem.at[m], zr_sem.at[m], device_id=partner, device_id_type=MESH
        )

    def scatter(m):
        mask = backwards(m, tp_bits)
        owner = peer(mask)
        if bit == 0:
            owner["rep"] = rep + lax.rem(lax.div(mask, 2), 2) * (other - rep)
        return pltpu.make_async_remote_copy(
            cast.at[m], arecv.at[m], as_sem.at[m], ar_sem.at[m], device_id=owner, device_id_type=MESH
        )

    def pass_on(source, via):
        land = flip(source, via, tp_bits) if not isinstance(source, int) else source ^ via
        return pltpu.make_async_remote_copy(
            packs.at[source], packs.at[land], ts_sem.at[land], tr_sem.at[land], device_id=peer(via), device_id_type=MESH
        )

    def arrival(m):
        return pltpu.make_async_remote_copy(
            packs.at[m], packs.at[m], ts_sem.at[m], tr_sem.at[m], device_id=peer(1), device_id_type=MESH
        )

    tok_in = pltpu.make_async_copy(tok_ref, packs.at[0, pl.ds(0, tok), :], t_in.at[0])
    cot_in = pltpu.make_async_copy(cot_ref, cot, t_in.at[1])
    last = blocks - 1

    @pl.loop(0, blocks)
    def _(i):
        load(last - i).start()

    tok_in.start()
    cot_in.start()

    barrier = pltpu.get_barrier_semaphore()
    pl.semaphore_signal(barrier, inc=1, device_id=partner, device_id_type=MESH)

    @pl.when(tp != 0)
    def _():
        pl.semaphore_signal(barrier, inc=1, device_id={"tp": 0}, device_id_type=MESH)

    def prepare(m):
        load(m).wait()
        zsend[m] = wbuf[m].astype(jnp.bfloat16)

    @pl.loop(0, AHEAD)
    def _(i):
        prepare(last - i)

    @pl.when(tp != 0)
    def _():
        pl.semaphore_wait(barrier, 1)

    @pl.when(tp == 0)
    def _():
        pl.semaphore_wait(barrier, blocks)
        if bit == 0:
            pl.semaphore_signal(all_sem, inc=1, device_id=partner, device_id_type=MESH)

    @pl.loop(0, AHEAD)
    def _(i):
        exchange(last - i).start()

    @pl.when(tp == 0)
    def _():
        if bit == 0:
            pl.semaphore_wait(all_sem, 1)

        @pl.loop(1, blocks)
        def _(t):
            pl.semaphore_signal(go_sem, inc=1, device_id={"tp": t}, device_id_type=MESH)

    tok_in.wait()
    cot_in.wait()
    for k in range(pieces):
        packs[0, pl.ds(tok, piece), pl.ds(k * LANES, LANES)] = cot[pl.ds(k * piece, piece), :]

    @pl.when(tp != 0)
    def _():
        pl.semaphore_wait(go_sem, 1)

    for via in (2, 12, 4, 1):
        pass_on(0, via).start()
    keys_acc[...] = jnp.zeros_like(keys_acc)
    ig_acc[...] = jnp.zeros_like(ig_acc)
    rate = LEARNING * (lax.rem(step_ref[0], 64) + 1).astype(jnp.float32) * (1.0 / 64.0)

    def average(i):
        m = last - i

        @pl.when(i + AHEAD < blocks)
        def _():
            prepare(m - AHEAD)
            exchange(m - AHEAD).start()

        exchange(m).wait_recv()
        mean = 0.5 * (wbuf[m] + zrecv[m].astype(jnp.float32))
        wbuf[m] = mean
        cast[m] = mean.astype(jnp.bfloat16)

        @pl.when(m > 0)
        def _():
            scatter(m).start()

    def project(m):
        block = packs[backwards(m, tp_bits), pl.ds(0, tok), :]
        keys_acc[...] += lax.dot_general(
            cast[m], block, (((1,), (1,)), ((), ())), preferred_element_type=jnp.float32
        )
        grad = jnp.dot(cot[...], block, preferred_element_type=jnp.float32)
        wbuf[m] = wbuf[m] - rate * grad
        store(m).start()

    def back(low):
        parts = []
        for q in range(4):
            m = backwards(low + q, tp_bits)
            for k in range(pieces):
                parts.append(packs[m, pl.ds(tok, piece), pl.ds(k * LANES, LANES)])
        left = jnp.concatenate(parts, axis=0)
        right = arecv[pl.ds(low, 4)].reshape(4 * features, width)
        ig_acc[...] += lax.dot_general(
            left, right, (((0,), (0,)), ((), ())), preferred_element_type=jnp.float32
        )

    @pl.loop(0, blocks)
    def _(i):
        average(i)
        for at, (source, vias) in zip(RELAY_STEPS, RELAYS):

            @pl.when(i == at)
            def _(source=source, vias=vias):
                arrival(source).wait_recv()
                for via in vias:
                    pass_on(source, via).start()

        @pl.when(i >= 12)
        def _():
            low = 4 * (last - i)

            @pl.when(i < 14)
            def _():
                for q in range(4):
                    arrival(backwards(low + q, tp_bits)).wait_recv()

            for q in range(4):
                project(low + 3 - q)

        @pl.when(i >= 13)
        def _():
            low = 4 * (blocks - i)
            for q in range(4):
                scatter(low + q).wait_recv()
            back(low)

    arecv[0] = cast[0]
    for q in range(1, 4):
        scatter(q).wait_recv()
    back(0)
    ig_ref[...] = ig_acc[...].astype(ig_ref.dtype)
    keys_ref[...] = keys_acc[...].astype(keys_ref.dtype)

    @pl.loop(0, blocks)
    def _(m):
        exchange(m).wait_send()
        store(m).wait()

        @pl.when(m > 0)
        def _():
            scatter(m).wait_send()
            arrival(m).wait_send()


def level(step_index, tokens, cot_t, weights, bit):
    blocks = lax.axis_size("tp")
    tok, width = tokens.shape
    features = cot_t.shape[0]
    rows = tok + features * LANES // width
    bf16, f32 = jnp.bfloat16, jnp.float32
    dma = pltpu.SemaphoreType.DMA((blocks,))
    hbm = pl.BlockSpec(memory_space=pl.ANY)
    vmem = pl.BlockSpec(memory_space=pltpu.VMEM)
    return pl.pallas_call(
        partial(kernel, bit),
        out_shape=(
            jax.ShapeDtypeStruct(weights.shape, f32),
            jax.ShapeDtypeStruct(cot_t.shape, bf16),
            jax.ShapeDtypeStruct(tokens.shape, bf16),
        ),
        in_specs=[pl.BlockSpec(memory_space=pltpu.SMEM), hbm, hbm, hbm],
        out_specs=(hbm, vmem, vmem),
        scratch_shapes=[
            pltpu.VMEM((blocks, features, width), f32),
            pltpu.VMEM((blocks, features, width), bf16),
            pltpu.VMEM((blocks, features, width), bf16),
            pltpu.VMEM((blocks, features, width), bf16),
            pltpu.VMEM((blocks, features, width), bf16),
            pltpu.VMEM((blocks, rows, width), bf16),
            pltpu.VMEM((features, tok), bf16),
            pltpu.VMEM((features, tok), f32),
            pltpu.VMEM((tok, width), f32),
            dma,
            dma,
            pltpu.SemaphoreType.DMA((2,)),
            dma,
            dma,
            dma,
            dma,
            dma,
            dma,
            pltpu.SemaphoreType.REGULAR,
            pltpu.SemaphoreType.REGULAR,
        ],
        compiler_params=pltpu.CompilerParams(
            collective_id=bit, has_side_effects=True, vmem_limit_bytes=32 * 2**20
        ),
    )(step_index, tokens, cot_t, weights)


def local(step_index, tokens, cotangent, weights):
    bits = lax.axis_size("rep").bit_length() - 1
    chosen = jnp.remainder(step_index[0], bits)
    branches = [partial(level, bit=bit) for bit in range(bits)]
    new_weights, keys_t, input_grad = lax.switch(chosen, branches, step_index, tokens, cotangent.T, weights)
    return (new_weights, keys_t.T, input_grad)


def solution(mesh):
    in_specs = (P(), P("rep", "tp"), P("rep", "tp"), P("rep", "tp", None))
    out_specs = (P("rep", "tp", None), P("rep", "tp"), P("rep", "tp"))
    return jax.shard_map(local, mesh=mesh, in_specs=in_specs, out_specs=out_specs, check_vma=False)
```

```python
from functools import partial

import jax
import jax.numpy as jnp
from jax import lax
from jax.experimental import pallas as pl
from jax.experimental.pallas import tpu as pltpu
from jax.sharding import PartitionSpec as P

LEARNING = 0.01
MESH = pl.DeviceIdType.MESH
LANES = 128
AHEAD = 8
RELAYS = ((2, (12, 4, 1)), (12, (4, 1)), (4, (1,)), (6, (12, 1)), (14, (1,)), (8, (1,)), (10, (1,)))
RELAY_STEPS = (3, 4, 5, 7, 8, 9, 10)


def flip(index, other, bits):
    out = 0
    for k in range(bits):
        a = lax.rem(lax.div(index, 2**k), 2)
        b = (other // 2**k) % 2 if isinstance(other, int) else lax.rem(lax.div(other, 2**k), 2)
        out = out + (a + b - 2 * a * b) * 2**k
    return out


def backwards(slot, bits):
    return sum(lax.rem(lax.div(jnp.int32(slot), 2**k), 2) * 2 ** (bits - 1 - k) for k in range(bits))


def kernel(
    bit,
    step_ref,
    tok_ref,
    cot_ref,
    w_ref,
    nw_ref,
    keys_ref,
    ig_ref,
    wbuf,
    zsend,
    zrecv,
    cast,
    arecv,
    packs,
    cot,
    keys_acc,
    ig_acc,
    w_sem,
    o_sem,
    t_in,
    zs_sem,
    zr_sem,
    as_sem,
    ar_sem,
    ts_sem,
    tr_sem,
    go_sem,
    all_sem,
    mid=None,
    hs_sem=None,
    hr_sem=None,
):
    blocks, features, width = wbuf.shape
    tok = tok_ref.shape[0]
    pieces = width // LANES
    piece = features // pieces
    tp = lax.axis_index("tp")
    rep = lax.axis_index("rep")
    tp_bits = blocks.bit_length() - 1
    rep_bits = lax.axis_size("rep").bit_length() - 1
    other = flip(rep, 2**bit, rep_bits)
    partner = {"rep": other}

    def peer(m):
        return {"tp": flip(tp, m, tp_bits)}

    def columns(s):
        return pl.ds(pl.multiple_of(flip(tp, backwards(s, tp_bits), tp_bits) * width, width), width)

    def load(m):
        return pltpu.make_async_copy(w_ref.at[0, :, columns(m)], wbuf.at[m], w_sem.at[m])

    def store(m):
        return pltpu.make_async_copy(wbuf.at[m], nw_ref.at[0, :, columns(m)], o_sem.at[m])

    def exchange(m):
        return pltpu.make_async_remote_copy(
            zsend.at[m], zrecv.at[m], zs_sem.at[m], zr_sem.at[m], device_id=partner, device_id_type=MESH
        )

    around = mid is not None
    turns = mid.shape[0] + 1 if around else 0
    apart = 2**bit // turns if around else 0
    ranks = lax.axis_size("rep")
    above, below = lax.rem(rep + apart, ranks), lax.rem(rep + ranks - apart, ranks)

    def hop(turn, s, first=False, final=False):
        up = lax.rem(jnp.int32(s), 2)
        return pltpu.make_async_remote_copy(
            zsend.at[s] if first else mid.at[turn - 1, s],
            zrecv.at[s] if final else mid.at[turn, s],
            hs_sem.at[turn, s],
            hr_sem.at[turn, s],
            device_id={"rep": up * above + (1 - up) * below},
            device_id_type=MESH,
        )

    def scatter(m):
        mask = backwards(m, tp_bits)
        owner = peer(mask)
        if bit == 0:
            owner["rep"] = rep + lax.rem(lax.div(mask, 2), 2) * (other - rep)
        return pltpu.make_async_remote_copy(
            cast.at[m], arecv.at[m], as_sem.at[m], ar_sem.at[m], device_id=owner, device_id_type=MESH
        )

    def pass_on(source, via):
        land = flip(source, via, tp_bits) if not isinstance(source, int) else source ^ via
        return pltpu.make_async_remote_copy(
            packs.at[source], packs.at[land], ts_sem.at[land], tr_sem.at[land], device_id=peer(via), device_id_type=MESH
        )

    def arrival(m):
        return pltpu.make_async_remote_copy(
            packs.at[m], packs.at[m], ts_sem.at[m], tr_sem.at[m], device_id=peer(1), device_id_type=MESH
        )

    tok_in = pltpu.make_async_copy(tok_ref, packs.at[0, pl.ds(0, tok), :], t_in.at[0])
    cot_in = pltpu.make_async_copy(cot_ref, cot, t_in.at[1])
    last = blocks - 1

    @pl.loop(0, blocks)
    def _(i):
        load(last - i).start()

    tok_in.start()
    cot_in.start()

    barrier = pltpu.get_barrier_semaphore()
    near = ({"rep": above}, {"rep": below}) if around else (partner,)
    for one in near:
        pl.semaphore_signal(barrier, inc=1, device_id=one, device_id_type=MESH)

    @pl.when(tp != 0)
    def _():
        pl.semaphore_signal(barrier, inc=1, device_id={"tp": 0}, device_id_type=MESH)

    def prepare(m):
        load(m).wait()
        zsend[m] = wbuf[m].astype(jnp.bfloat16)

    ahead = blocks if around else AHEAD

    @pl.loop(0, ahead)
    def _(i):
        prepare(last - i)

    @pl.when(tp != 0)
    def _():
        pl.semaphore_wait(barrier, len(near))

    @pl.when(tp == 0)
    def _():
        pl.semaphore_wait(barrier, blocks - 1 + len(near))
        if bit == 0:
            pl.semaphore_signal(all_sem, inc=1, device_id=partner, device_id_type=MESH)

    @pl.loop(0, ahead)
    def _(i):
        if around:
            hop(0, last - i, first=True).start()
        else:
            exchange(last - i).start()

    @pl.when(tp == 0)
    def _():
        if bit == 0:
            pl.semaphore_wait(all_sem, 1)

        @pl.loop(1, blocks)
        def _(t):
            pl.semaphore_signal(go_sem, inc=1, device_id={"tp": t}, device_id_type=MESH)

    tok_in.wait()
    cot_in.wait()
    for k in range(pieces):
        packs[0, pl.ds(tok, piece), pl.ds(k * LANES, LANES)] = cot[pl.ds(k * piece, piece), :]

    @pl.when(tp != 0)
    def _():
        pl.semaphore_wait(go_sem, 1)

    for via in (2, 12, 4, 1):
        pass_on(0, via).start()
    keys_acc[...] = jnp.zeros_like(keys_acc)
    ig_acc[...] = jnp.zeros_like(ig_acc)
    rate = LEARNING * (lax.rem(step_ref[0], 64) + 1).astype(jnp.float32) * (1.0 / 64.0)

    def average(i):
        m = last - i

        if around:
            hop(turns - 1, m, final=True).wait_recv()
        else:

            @pl.when(i + AHEAD < blocks)
            def _():
                prepare(m - AHEAD)
                exchange(m - AHEAD).start()

            exchange(m).wait_recv()

        mean = 0.5 * (wbuf[m] + zrecv[m].astype(jnp.float32))
        wbuf[m] = mean
        cast[m] = mean.astype(jnp.bfloat16)

        @pl.when(m > 0)
        def _():
            scatter(m).start()

    def project(m):
        block = packs[backwards(m, tp_bits), pl.ds(0, tok), :]
        keys_acc[...] += lax.dot_general(
            cast[m], block, (((1,), (1,)), ((), ())), preferred_element_type=jnp.float32
        )
        grad = jnp.dot(cot[...], block, preferred_element_type=jnp.float32)
        wbuf[m] = wbuf[m] - rate * grad
        store(m).start()

    def back(low):
        parts = []
        for q in range(4):
            m = backwards(low + q, tp_bits)
            for k in range(pieces):
                parts.append(packs[m, pl.ds(tok, piece), pl.ds(k * LANES, LANES)])
        left = jnp.concatenate(parts, axis=0)
        right = arecv[pl.ds(low, 4)].reshape(4 * features, width)
        ig_acc[...] += lax.dot_general(
            left, right, (((0,), (0,)), ((), ())), preferred_element_type=jnp.float32
        )

    def relays(i):
        for at, (source, vias) in zip(RELAY_STEPS, RELAYS):

            @pl.when(i == at)
            def _(source=source, vias=vias):
                arrival(source).wait_recv()
                for via in vias:
                    pass_on(source, via).start()

    if around:

        @pl.loop(1, turns - 1)
        def _(turn):
            @pl.loop(0, blocks)
            def _(i):
                hop(turn - 1, last - i, first=True).wait_recv()
                hop(turn, last - i).start()

                @pl.when(turn == 2)
                def _():
                    relays(i)

        @pl.loop(0, blocks)
        def _(i):
            hop(turns - 2, last - i, first=True).wait_recv()
            hop(turns - 1, last - i, final=True).start()

    @pl.loop(0, blocks)
    def _(i):
        average(i)
        if not around:
            relays(i)

        @pl.when(i >= 12)
        def _():
            low = 4 * (last - i)

            @pl.when(i < 14)
            def _():
                for q in range(4):
                    arrival(backwards(low + q, tp_bits)).wait_recv()

            for q in range(4):
                project(low + 3 - q)

        @pl.when(i >= 13)
        def _():
            low = 4 * (blocks - i)
            for q in range(4):
                scatter(low + q).wait_recv()
            back(low)

    arecv[0] = cast[0]
    for q in range(1, 4):
        scatter(q).wait_recv()
    back(0)
    ig_ref[...] = ig_acc[...].astype(ig_ref.dtype)
    keys_ref[...] = keys_acc[...].astype(keys_ref.dtype)

    @pl.loop(0, blocks)
    def _(m):
        if around:

            @pl.loop(0, turns - 1)
            def _(turn):
                hop(turn, m, first=True).wait_send()

            hop(turns - 1, m, final=True).wait_send()
        else:
            exchange(m).wait_send()

        store(m).wait()

        @pl.when(m > 0)
        def _():
            scatter(m).wait_send()
            arrival(m).wait_send()


def level(step_index, tokens, cot_t, weights, bit):
    blocks = lax.axis_size("tp")
    tok, width = tokens.shape
    features = cot_t.shape[0]
    rows = tok + features * LANES // width
    bf16, f32 = jnp.bfloat16, jnp.float32
    dma = pltpu.SemaphoreType.DMA((blocks,))
    hbm = pl.BlockSpec(memory_space=pl.ANY)
    vmem = pl.BlockSpec(memory_space=pltpu.VMEM)
    ranks = lax.axis_size("rep")
    turns = ranks // 4
    extra = []
    if 2**bit == ranks // 2:
        extra = [
            pltpu.VMEM((turns - 1, blocks, features, width), bf16),
            pltpu.SemaphoreType.DMA((turns, blocks)),
            pltpu.SemaphoreType.DMA((turns, blocks)),
        ]
    return pl.pallas_call(
        partial(kernel, bit),
        out_shape=(
            jax.ShapeDtypeStruct(weights.shape, f32),
            jax.ShapeDtypeStruct(cot_t.shape, bf16),
            jax.ShapeDtypeStruct(tokens.shape, bf16),
        ),
        in_specs=[pl.BlockSpec(memory_space=pltpu.SMEM), hbm, hbm, hbm],
        out_specs=(hbm, vmem, vmem),
        scratch_shapes=[
            pltpu.VMEM((blocks, features, width), f32),
            pltpu.VMEM((blocks, features, width), bf16),
            pltpu.VMEM((blocks, features, width), bf16),
            pltpu.VMEM((blocks, features, width), bf16),
            pltpu.VMEM((blocks, features, width), bf16),
            pltpu.VMEM((blocks, rows, width), bf16),
            pltpu.VMEM((features, tok), bf16),
            pltpu.VMEM((features, tok), f32),
            pltpu.VMEM((tok, width), f32),
            dma,
            dma,
            pltpu.SemaphoreType.DMA((2,)),
            dma,
            dma,
            dma,
            dma,
            dma,
            dma,
            pltpu.SemaphoreType.REGULAR,
            pltpu.SemaphoreType.REGULAR,
            *extra,
        ],
        compiler_params=pltpu.CompilerParams(
            collective_id=bit, has_side_effects=True, vmem_limit_bytes=32 * 2**20
        ),
    )(step_index, tokens, cot_t, weights)


def local(step_index, tokens, cotangent, weights):
    bits = lax.axis_size("rep").bit_length() - 1
    chosen = jnp.remainder(step_index[0], bits)
    branches = [partial(level, bit=bit) for bit in range(bits)]
    new_weights, keys_t, input_grad = lax.switch(chosen, branches, step_index, tokens, cotangent.T, weights)
    return (new_weights, keys_t.T, input_grad)


def solution(mesh):
    in_specs = (P(), P("rep", "tp"), P("rep", "tp"), P("rep", "tp", None))
    out_specs = (P("rep", "tp", None), P("rep", "tp"), P("rep", "tp"))
    return jax.shard_map(local, mesh=mesh, in_specs=in_specs, out_specs=out_specs, check_vma=False)
```
